32 devices in a mesh: pipe: 4 (over x, core), tensor: 8 (over z, y).
Axes of the slice: x: 2, y: 2, z: 4, core: 2. Of those that a mesh axis runs over, the one named last changes fastest.
Arguments:
- queries: bfloat16 [8, 64, 16384], P('pipe', None, 'tensor'), may hold values from -10 to 10
- stored_keys: bfloat16 [8, 8192, 1024], P('pipe', 'tensor'), may hold values from -5 to 5
- stored_values: bfloat16 [8, 8192, 1024], P('pipe', 'tensor'), may hold values from -6 to 6
- node_keys: bfloat16 [8, 64, 1024], P('pipe'), may hold values from -10 to 10
- node_values: bfloat16 [8, 64, 1024], P('pipe'), may hold values from -6 to 6
- parents: int32 [8, 64], P('pipe'), may hold values from 0 to 62, as said below
- lengths: int32 [8], P('pipe'), may hold values from 4096 to 8192, as said below
Outputs:
- passed: bfloat16 [8, 64, 16384], P('pipe', None, 'tensor')
The draws below stay inside these ranges and needn't reach their ends.
Inputs may be any that keep to these rules, and one draw needn't show every extreme that they name: `parents`: node 0 is the root and its entry is 0; the parent of every other node has a lower index, one to four below it or 0; the last node's parent is the node before it. `lengths`: in every draw some request has exactly 8192 live positions and some exactly 4096.
All inputs are finite; a program needn't handle non-finite values.
Results may differ from the reference program's by a relative error of at most 0.01045.
Values may be sent and summed in bfloat16 or wider, within the bound.
A program may use at most 128 MiB of HBM per device.

```python
import jax
import jax.numpy as jnp
from jax import lax

QUERY_HEADS = 128
KEY_VALUE_HEADS = 8
HEAD_SIZE = 128
TREE_NODES = 64
REQ = 2
DEVICE_POSITIONS = 1024
REQUEST_COUNT = 8
CACHE_LENGTH = 8192
KVW = 1024
N_PIPE = 4
N_TENSOR = 8


def draw_queries(key, part):
    key = jax.random.fold_in(key, 31)
    array_shape = (REQUEST_COUNT, TREE_NODES, QUERY_HEADS * HEAD_SIZE)
    values = jnp.clip(2.5 * jax.random.normal(key, array_shape, jnp.float32), -10.0, 10.0)
    return values.astype(jnp.bfloat16)


def draw_stored_keys(key, part):
    key = jax.random.fold_in(key, 32)
    array_shape = (REQUEST_COUNT, CACHE_LENGTH, KEY_VALUE_HEADS * HEAD_SIZE)
    values = jnp.clip(jax.random.normal(key, array_shape, jnp.float32), -5.0, 5.0)
    return values.astype(jnp.bfloat16)


def draw_parents(key, part):
    key = jax.random.fold_in(key, 33)
    offsets = jax.random.randint(key, (REQUEST_COUNT, TREE_NODES), 0, 4)
    node_index = jnp.arange(TREE_NODES, dtype=jnp.int32)[None, :]
    parent = jnp.maximum(node_index - 1 - offsets, 0)
    parent = jnp.where(node_index == TREE_NODES - 1, TREE_NODES - 2, parent)
    return parent.astype(jnp.int32)


def draw_lengths(key, part):
    key = jax.random.fold_in(key, 34)
    first_key, second_key, third_key = jax.random.split(key, 3)
    values = jax.random.randint(first_key, (REQUEST_COUNT,), CACHE_LENGTH // 2, CACHE_LENGTH + 1)
    longest = jax.random.randint(second_key, (), 0, REQUEST_COUNT)
    shortest = (longest + 1 + jax.random.randint(third_key, (), 0, REQUEST_COUNT - 1)) % REQUEST_COUNT
    request_index = jnp.arange(REQUEST_COUNT)
    values = jnp.where(request_index == longest, CACHE_LENGTH, jnp.where(request_index == shortest, CACHE_LENGTH // 2, values))
    return values.astype(jnp.int32)


def steps_of(rng, extent, pieces, smallest, top_value):
    gain = 1.0
    for dim, blocks in pieces:
        steps = jax.random.uniform(jax.random.fold_in(jax.random.fold_in(rng, 6), dim), (blocks,), jnp.float32, smallest / len(pieces), top_value / len(pieces))
        gain = gain * jnp.repeat(jnp.exp(steps), extent[dim] // blocks).reshape((-1,) + (1,) * (len(extent) - 1 - dim))
    return gain


def gaussian(stream_key, extent, width, limit, shards=(), held_as=jnp.bfloat16):
    gain = steps_of(stream_key, extent, shards, -0.22, 0.18) if shards else 1.0
    entries = jax.random.normal(stream_key, extent, jnp.float32) * width * gain
    return jnp.minimum(jnp.maximum(entries, -limit), limit).astype(held_as)


def setup_inputs(seed: int = 0) -> dict:
    keys = jax.random.split(jax.random.key(seed), 8)
    return {
        "queries": draw_queries(jax.random.fold_in(keys[7], 71), 0),
        "stored_keys": draw_stored_keys(jax.random.fold_in(keys[7], 71), 0),
        "stored_values": gaussian(keys[2], (REQUEST_COUNT, CACHE_LENGTH, KVW), 1.0, 6.0, ((0, 4), (1, 8))),
        "node_keys": gaussian(keys[3], (REQUEST_COUNT, TREE_NODES, KVW), 1.7, 10.0, ((0, 4),)),
        "node_values": gaussian(keys[4], (REQUEST_COUNT, TREE_NODES, KVW), 1.0, 6.0, ((0, 4),)),
        "parents": draw_parents(jax.random.fold_in(keys[7], 71), 0),
        "lengths": draw_lengths(jax.random.fold_in(keys[7], 71), 0),
    }


MASKED_SCORE = -1e30


def ancestry(parents):
    tree_node_count = parents.shape[-1]
    node_index = jnp.arange(tree_node_count, dtype=jnp.int32)
    reached = (parents[..., :, None] == node_index).astype(jnp.float32)
    reached = jnp.maximum(reached, jnp.eye(tree_node_count, dtype=jnp.float32))
    for squaring in range(tree_node_count.bit_length()):
        product = jnp.einsum("...ij,...jk->...ik", reached, reached, precision=lax.Precision.HIGHEST)
        reached = (product > 0.5).astype(jnp.float32)
    return reached > 0.5


def block_partial(query_row_slice, key_row_slice, value_row_slice, active_mask):
    scale = query_row_slice.shape[-1] ** -0.5
    scores = jnp.dot(query_row_slice.astype(jnp.float32), key_row_slice.astype(jnp.float32).T, precision=lax.Precision.HIGHEST) * scale
    masked = jnp.where(active_mask[None, :], scores, MASKED_SCORE)
    row_max = jnp.max(masked, axis=1)
    exponent = jnp.where(active_mask[None, :], jnp.exp(masked - row_max[:, None]), 0.0)
    row_sum = jnp.sum(exponent, axis=1)
    rounded = lax.optimization_barrier(exponent.astype(jnp.bfloat16))
    numerator = jnp.dot(rounded.astype(jnp.float32), value_row_slice.astype(jnp.float32), precision=lax.Precision.HIGHEST)
    output = (numerator / jnp.maximum(row_sum, 1.0)[:, None]).astype(jnp.bfloat16)
    return row_max, row_sum, output


def tree_partial(query_row_slice, key_row_slice, value_row_slice, allowed):
    scale = query_row_slice.shape[-1] ** -0.5
    scores = jnp.dot(query_row_slice.astype(jnp.float32), key_row_slice.astype(jnp.float32).T, precision=lax.Precision.HIGHEST) * scale
    masked = jnp.where(allowed, scores, MASKED_SCORE)
    row_max = jnp.max(masked, axis=1)
    exponent = jnp.where(allowed, jnp.exp(masked - row_max[:, None]), 0.0)
    row_sum = jnp.sum(exponent, axis=1)
    rounded = lax.optimization_barrier(exponent.astype(jnp.bfloat16))
    numerator = jnp.dot(rounded.astype(jnp.float32), value_row_slice.astype(jnp.float32), precision=lax.Precision.HIGHEST)
    return row_max, row_sum, numerator / row_sum[:, None]


def one_request(operands):
    query_input, key_collection, value_collection, node_key_collection, node_value_collection, parent, length = operands
    query_group_size = QUERY_HEADS // KEY_VALUE_HEADS
    query_row_slice = query_input.reshape(TREE_NODES, KEY_VALUE_HEADS, query_group_size, HEAD_SIZE).transpose(1, 0, 2, 3).reshape(KEY_VALUE_HEADS, TREE_NODES * query_group_size, HEAD_SIZE)
    key_block_list = key_collection.reshape(N_TENSOR, DEVICE_POSITIONS, KEY_VALUE_HEADS, HEAD_SIZE).transpose(2, 0, 1, 3)
    value_block_list = value_collection.reshape(N_TENSOR, DEVICE_POSITIONS, KEY_VALUE_HEADS, HEAD_SIZE).transpose(2, 0, 1, 3)
    node_key_rows = node_key_collection.reshape(TREE_NODES, KEY_VALUE_HEADS, HEAD_SIZE).transpose(1, 0, 2)
    node_value_rows = node_value_collection.reshape(TREE_NODES, KEY_VALUE_HEADS, HEAD_SIZE).transpose(1, 0, 2)
    active_mask = (jnp.arange(CACHE_LENGTH, dtype=jnp.int32) < length).reshape(N_TENSOR, DEVICE_POSITIONS)
    allowed = jnp.repeat(ancestry(parent), query_group_size, axis=0)

    def per_head(head_operands):
        head_query, head_keys, head_values, head_tree_keys, head_tree_values = head_operands
        block_running_max, block_exp_sum, block_result_rows = jax.vmap(block_partial, in_axes=(None, 0, 0, 0))(head_query, head_keys, head_values, active_mask)
        tree_max, tree_sum, tree_out = tree_partial(head_query, head_tree_keys, head_tree_values, allowed)
        row_best = jnp.maximum(tree_max, jnp.max(block_running_max, axis=0))
        tree_weight = tree_sum * jnp.exp(tree_max - row_best)
        block_weight = block_exp_sum * jnp.exp(block_running_max - row_best[None, :])
        numerator = tree_weight[:, None] * tree_out + jnp.sum(block_weight[..., None] * block_result_rows.astype(jnp.float32), axis=0)
        denominator = tree_weight + jnp.sum(block_weight, axis=0)
        return (numerator / denominator[:, None]).astype(jnp.bfloat16)

    final_output = lax.map(per_head, (query_row_slice, key_block_list, value_block_list, node_key_rows, node_value_rows))
    return final_output.reshape(KEY_VALUE_HEADS, TREE_NODES, query_group_size, HEAD_SIZE).transpose(1, 0, 2, 3).reshape(TREE_NODES, QUERY_HEADS * HEAD_SIZE)


def reference(queries, stored_keys, stored_values, node_keys, node_values, parents, lengths):
    attended = lax.map(one_request, (queries, stored_keys, stored_values, node_keys, node_values, parents, lengths))
    sectioned = attended.reshape(N_PIPE, REQ, TREE_NODES, QUERY_HEADS * HEAD_SIZE)
    return jnp.roll(sectioned, 1, axis=0).reshape(REQUEST_COUNT, TREE_NODES, QUERY_HEADS * HEAD_SIZE)
```

```python
import functools

import jax
import jax.numpy as jnp
from jax import lax
from jax.experimental import pallas as pl
from jax.experimental.pallas import tpu as pltpu
from jax.sharding import PartitionSpec as P

QUERY_HEADS = 128
KEY_VALUE_HEADS = 8
HEAD_SIZE = 128
MASKED_SCORE = -1e30
NT = (((1,), (1,)), ((), ()))
TN = (((0,), (0,)), ((), ()))


def head_rows(block):
    heads = block.shape[1] // HEAD_SIZE
    return jnp.concatenate(
        [block[:, h * HEAD_SIZE : (h + 1) * HEAD_SIZE] for h in range(heads)], axis=0
    )


def block_kernel(first_ref, lengths_ref, q_ref, k_ref, v_ref, o_ref, stat_ref):
    live = lengths_ref[pl.program_id(0)] - first_ref[0]
    keys = k_ref[0]
    values = v_ref[0]
    positions = lax.broadcasted_iota(jnp.int32, (keys.shape[0], 1), 0)
    active = positions < live
    scale = HEAD_SIZE**-0.5
    for part in range(q_ref.shape[0]):
        heads = q_ref.shape[3] // HEAD_SIZE
        for first in range(0, heads, 4):
            rows = head_rows(q_ref[part, 0, :, first * HEAD_SIZE : (first + 4) * HEAD_SIZE])
            scores = lax.dot_general(keys, rows, NT, preferred_element_type=jnp.float32)
            scores = jnp.where(active, scores * scale, MASKED_SCORE)
            top = jnp.max(scores, axis=0, keepdims=True)
            weights = jnp.exp(scores - top)
            total = jnp.sum(weights, axis=0, keepdims=True)
            out = lax.dot_general(
                values, weights.astype(jnp.bfloat16), TN, preferred_element_type=jnp.float32
            )
            columns = slice(first * 64, (first + 4) * 64)
            o_ref[part, 0, :, columns] = (out / total).astype(jnp.bfloat16)
            stat_ref[part, 0, 0:1, columns] = top
            stat_ref[part, 0, 1:2, columns] = total


def block_attention(queries, keys, values, first, lengths):
    ranks, requests, nodes, width = queries.shape
    extent = keys.shape[1]
    share = ranks // KEY_VALUE_HEADS
    rows = width // HEAD_SIZE * nodes
    return pl.pallas_call(
        block_kernel,
        grid=(requests, KEY_VALUE_HEADS),
        in_specs=[
            pl.BlockSpec(memory_space=pltpu.SMEM),
            pl.BlockSpec(memory_space=pltpu.SMEM),
            pl.BlockSpec((share, 1, nodes, width), lambda r, g: (g, r, 0, 0)),
            pl.BlockSpec((1, extent, HEAD_SIZE), lambda r, g: (r, 0, g)),
            pl.BlockSpec((1, extent, HEAD_SIZE), lambda r, g: (r, 0, g)),
        ],
        out_specs=[
            pl.BlockSpec((share, 1, HEAD_SIZE, rows), lambda r, g: (g, r, 0, 0)),
            pl.BlockSpec((share, 1, 2, rows), lambda r, g: (g, r, 0, 0)),
        ],
        out_shape=[
            jax.ShapeDtypeStruct((ranks, requests, HEAD_SIZE, rows), jnp.bfloat16),
            jax.ShapeDtypeStruct((ranks, requests, 2, rows), jnp.float32),
        ],
        compiler_params=pltpu.CompilerParams(vmem_limit_bytes=40 << 20),
    )(first, lengths, queries, keys, values)


def tree_part(rows, node_keys, node_values, parents):
    nodes = node_keys.shape[0]
    row = lax.broadcasted_iota(jnp.int32, (nodes, nodes), 0)
    column = lax.broadcasted_iota(jnp.int32, (nodes, nodes), 1)
    reached = ((parents == row) | (row == column)).astype(jnp.bfloat16)
    for squaring in range(nodes.bit_length()):
        product = jnp.dot(reached, reached, preferred_element_type=jnp.float32)
        reached = (product > 0.5).astype(jnp.bfloat16)
    width = rows.shape[0]
    node = lax.broadcasted_iota(jnp.int32, (nodes, width), 0)
    owner = lax.rem(lax.broadcasted_iota(jnp.int32, (nodes, width), 1), nodes)
    spread = (node == owner).astype(jnp.bfloat16)
    allowed = jnp.dot(reached, spread, preferred_element_type=jnp.float32) > 0.5
    scores = lax.dot_general(node_keys, rows, NT, preferred_element_type=jnp.float32)
    scores = jnp.where(allowed, scores * HEAD_SIZE**-0.5, MASKED_SCORE)
    top = jnp.max(scores, axis=0, keepdims=True)
    weights = jnp.where(allowed, jnp.exp(scores - top), 0.0)
    total = jnp.sum(weights, axis=0, keepdims=True)
    out = lax.dot_general(
        node_values, weights.astype(jnp.bfloat16), TN, preferred_element_type=jnp.float32
    )
    return top, total, out / total


def join_kernel(q_ref, nk_ref, nv_ref, parents_ref, summed_ref, stat_ref, out_ref):
    nodes = q_ref.shape[1]
    top, total, tree = tree_part(head_rows(q_ref[0]), nk_ref[0], nv_ref[0], parents_ref[0])
    block_top, block_total = stat_ref[0, 0:1], stat_ref[0, 1:2]
    best = jnp.maximum(top, block_top)
    a = total * jnp.exp(top - best)
    c = block_total * jnp.exp(block_top - best)
    joined = (a * tree + c * summed_ref[0].astype(jnp.float32)) / (a + c)
    joined = joined.T.astype(out_ref.dtype)
    for h in range(q_ref.shape[2] // HEAD_SIZE):
        out_ref[0, :, h * HEAD_SIZE : (h + 1) * HEAD_SIZE] = joined[h * nodes : (h + 1) * nodes]


def join(queries, node_keys, node_values, parents, summed, stats):
    def one(x):
        return pl.BlockSpec((1,) + x.shape[1:], lambda r: (r,) + (0,) * (x.ndim - 1))

    operands = (queries, node_keys, node_values, parents[:, None, :], summed, stats)
    return pl.pallas_call(
        join_kernel,
        grid=(queries.shape[0],),
        in_specs=[one(x) for x in operands],
        out_specs=one(queries),
        out_shape=jax.ShapeDtypeStruct(queries.shape, jnp.bfloat16),
        compiler_params=pltpu.CompilerParams(vmem_limit_bytes=32 << 20),
    )(*operands)


def per_device(queries, stored_keys, stored_values, node_keys, node_values, parents, lengths):
    ranks = lax.axis_size("tensor")
    rank = lax.axis_index("tensor")
    extent = stored_keys.shape[1]
    every = lax.all_gather(queries, "tensor", axis=0, tiled=False)
    first = (rank * extent).astype(jnp.int32)[None]
    outs, stats = block_attention(every, stored_keys, stored_values, first, lengths)
    every_stat = lax.all_gather(stats, "tensor", axis=0, tiled=False)
    best = jnp.max(every_stat[:, :, :, 0], axis=0)
    total = jnp.sum(every_stat[:, :, :, 1] * jnp.exp(every_stat[:, :, :, 0] - best), axis=0)
    fraction = stats[:, :, 1] * jnp.exp(stats[:, :, 0] - best) / total
    weighted = (outs.astype(jnp.float32) * fraction[:, :, None, :]).astype(jnp.bfloat16)
    summed = lax.psum_scatter(weighted, "tensor", scatter_dimension=0, tiled=False)
    own_stats = lax.dynamic_index_in_dim(jnp.stack([best, total], axis=2), rank, 0, keepdims=False)
    group = rank * KEY_VALUE_HEADS // ranks
    own_keys = lax.dynamic_slice_in_dim(node_keys, group * HEAD_SIZE, HEAD_SIZE, 2)
    own_values = lax.dynamic_slice_in_dim(node_values, group * HEAD_SIZE, HEAD_SIZE, 2)
    attended = join(queries, own_keys, own_values, parents, summed, own_stats)
    length = lax.axis_size("pipe")
    return lax.ppermute(attended, "pipe", [(i, (i + 1) % length) for i in range(length)])


def solution(mesh):
    placed = (
        P("pipe", None, "tensor"),
        P("pipe", "tensor", None),
        P("pipe", "tensor", None),
        P("pipe", None, None),
        P("pipe", None, None),
        P("pipe", None),
        P("pipe"),
    )
    return jax.shard_map(
        per_device, mesh=mesh, in_specs=placed, out_specs=P("pipe", None, "tensor"), check_vma=False
    )
```

```python
import functools

import jax
import jax.numpy as jnp
from jax import lax
from jax.experimental import pallas as pl
from jax.experimental.pallas import tpu as pltpu
from jax.sharding import PartitionSpec as P

QUERY_HEADS = 128
KEY_VALUE_HEADS = 8
HEAD_SIZE = 128
MASKED_SCORE = -1e30
LOG2_E = 1.4426950408889634
NT = (((1,), (1,)), ((), ()))
TN = (((0,), (0,)), ((), ()))


def head_rows(block):
    heads = block.shape[1] // HEAD_SIZE
    return jnp.concatenate(
        [block[:, h * HEAD_SIZE : (h + 1) * HEAD_SIZE] for h in range(heads)], axis=0
    )


def block_kernel(first_ref, lengths_ref, q_ref, k_ref, v_ref, o_ref, stat_ref):
    live = lengths_ref[pl.program_id(0)] - first_ref[0]
    keys = k_ref[0]
    values = v_ref[0]
    positions = lax.broadcasted_iota(jnp.int32, (keys.shape[0], 1), 0)
    active = positions < live
    scale = HEAD_SIZE**-0.5
    for part in range(q_ref.shape[0]):
        heads = q_ref.shape[3] // HEAD_SIZE
        for first in range(0, heads, 4):
            rows = head_rows(q_ref[part, 0, :, first * HEAD_SIZE : (first + 4) * HEAD_SIZE])
            scores = lax.dot_general(keys, rows, NT, preferred_element_type=jnp.float32)
            scores = jnp.where(active, scores, MASKED_SCORE)
            top = jnp.max(scores, axis=0, keepdims=True)
            weights = jnp.exp2((scores - top) * (scale * LOG2_E))
            total = jnp.sum(weights, axis=0, keepdims=True)
            out = lax.dot_general(
                values, weights.astype(jnp.bfloat16), TN, preferred_element_type=jnp.float32
            )
            columns = slice(first * 64, (first + 4) * 64)
            o_ref[part, 0, :, columns] = (out / total).astype(jnp.bfloat16)
            stat_ref[part, 0, 0:1, columns] = top * scale
            stat_ref[part, 0, 1:2, columns] = total


def block_attention(queries, keys, values, first, lengths):
    ranks, requests, nodes, width = queries.shape
    extent = keys.shape[1]
    share = ranks // KEY_VALUE_HEADS
    rows = width // HEAD_SIZE * nodes
    return pl.pallas_call(
        block_kernel,
        grid=(requests, KEY_VALUE_HEADS),
        in_specs=[
            pl.BlockSpec(memory_space=pltpu.SMEM),
            pl.BlockSpec(memory_space=pltpu.SMEM),
            pl.BlockSpec((share, 1, nodes, width), lambda r, g: (g, r, 0, 0)),
            pl.BlockSpec((1, extent, HEAD_SIZE), lambda r, g: (r, 0, g)),
            pl.BlockSpec((1, extent, HEAD_SIZE), lambda r, g: (r, 0, g)),
        ],
        out_specs=[
            pl.BlockSpec((share, 1, HEAD_SIZE, rows), lambda r, g: (g, r, 0, 0)),
            pl.BlockSpec((share, 1, 2, rows), lambda r, g: (g, r, 0, 0)),
        ],
        out_shape=[
            jax.ShapeDtypeStruct((ranks, requests, HEAD_SIZE, rows), jnp.bfloat16),
            jax.ShapeDtypeStruct((ranks, requests, 2, rows), jnp.float32),
        ],
        compiler_params=pltpu.CompilerParams(vmem_limit_bytes=40 << 20),
    )(first, lengths, queries, keys, values)


def tree_part(rows, node_keys, node_values, parents):
    nodes = node_keys.shape[0]
    row = lax.broadcasted_iota(jnp.int32, (nodes, nodes), 0)
    column = lax.broadcasted_iota(jnp.int32, (nodes, nodes), 1)
    reached = ((parents == row) | (row == column)).astype(jnp.bfloat16)
    for squaring in range(nodes.bit_length()):
        product = jnp.dot(reached, reached, preferred_element_type=jnp.float32)
        reached = (product > 0.5).astype(jnp.bfloat16)
    width = rows.shape[0]
    node = lax.broadcasted_iota(jnp.int32, (nodes, width), 0)
    owner = lax.rem(lax.broadcasted_iota(jnp.int32, (nodes, width), 1), nodes)
    spread = (node == owner).astype(jnp.bfloat16)
    allowed = jnp.dot(reached, spread, preferred_element_type=jnp.float32) > 0.5
    scores = lax.dot_general(node_keys, rows, NT, preferred_element_type=jnp.float32)
    scores = jnp.where(allowed, scores * HEAD_SIZE**-0.5, MASKED_SCORE)
    top = jnp.max(scores, axis=0, keepdims=True)
    weights = jnp.where(allowed, jnp.exp(scores - top), 0.0)
    total = jnp.sum(weights, axis=0, keepdims=True)
    out = lax.dot_general(
        node_values, weights.astype(jnp.bfloat16), TN, preferred_element_type=jnp.float32
    )
    return top, total, out / total


def peer(z, y, across):
    return {"tensor": z * across + y}


def remote(source, target, sends, receives, at, device):
    return pltpu.make_async_remote_copy(
        src_ref=source,
        dst_ref=target,
        send_sem=sends.at[at],
        recv_sem=receives.at[at],
        device_id=device,
        device_id_type=pl.DeviceIdType.MESH,
    )


def greet(deep, across, z, y):
    barrier = pltpu.get_barrier_semaphore()
    partners = [peer(lax.rem(z + dz, deep), y, across) for dz in range(1, deep)]
    partners += [peer(z, lax.rem(y + dy, across), across) for dy in range(1, across)]
    for partner in partners:
        pl.semaphore_signal(
            barrier, inc=1, device_id=partner, device_id_type=pl.DeviceIdType.MESH
        )
    pl.semaphore_wait(barrier, len(partners))


def gather_kernel(
    deep, across, q_ref, every_ref, own_sem, z_send, z_receive, y_send, y_receive
):
    rank = lax.axis_index("tensor")
    z, y = rank // across, lax.rem(rank, across)
    greet(deep, across, z, y)
    requests = q_ref.shape[0]
    own = pltpu.make_async_copy(q_ref, every_ref.at[rank], own_sem)
    own.start()
    along_z, along_y = [], []
    for r in range(requests):
        for dz in range(1, deep):
            copy = remote(
                q_ref.at[r],
                every_ref.at[rank, r],
                z_send,
                z_receive,
                (r, dz - 1),
                peer(lax.rem(z + dz, deep), y, across),
            )
            copy.start()
            along_z.append(copy)
        for dy in range(1, across):
            copy = remote(
                q_ref.at[r],
                every_ref.at[rank, r],
                y_send,
                y_receive,
                (r, 0, dy - 1),
                peer(z, lax.rem(y + dy, across), across),
            )
            copy.start()
            along_y.append(copy)
    for r in range(requests):
        for dz in range(1, deep):
            source = lax.rem(z + deep - dz, deep) * across + y
            remote(
                q_ref.at[r], every_ref.at[source, r], z_send, z_receive, (r, dz - 1),
                peer(lax.rem(z + dz, deep), y, across),
            ).wait_recv()
            for dy in range(1, across):
                copy = remote(
                    every_ref.at[source, r],
                    every_ref.at[source, r],
                    y_send,
                    y_receive,
                    (r, dz, dy - 1),
                    peer(z, lax.rem(y + dy, across), across),
                )
                copy.start()
                along_y.append(copy)
    for copy in along_z:
        copy.wait_send()
    for copy in along_y:
        copy.wait()
    own.wait()


def gather(queries, ranks):
    deep = 4
    across = ranks // deep
    requests = queries.shape[0]
    semaphore = pltpu.SemaphoreType.DMA
    return pl.pallas_call(
        functools.partial(gather_kernel, deep, across),
        in_specs=[pl.BlockSpec(memory_space=pltpu.VMEM)],
        out_specs=pl.BlockSpec(memory_space=pltpu.VMEM),
        out_shape=jax.ShapeDtypeStruct((ranks,) + queries.shape, queries.dtype),
        scratch_shapes=[
            semaphore,
            semaphore((requests, deep - 1)),
            semaphore((requests, deep - 1)),
            semaphore((requests, deep, across - 1)),
            semaphore((requests, deep, across - 1)),
        ],
        compiler_params=pltpu.CompilerParams(
            collective_id=0, has_side_effects=True, vmem_limit_bytes=32 << 20
        ),
    )(queries)


def combine(parts):
    best = functools.reduce(jnp.maximum, [top for top, total, mean in parts])
    shares = [total * jnp.exp(top - best) for top, total, mean in parts]
    whole = sum(shares[1:], shares[0])
    mean = sum(
        (share / whole) * part[2].astype(jnp.float32) for share, part in zip(shares, parts)
    )
    return best, whole, mean


def join_kernel(
    deep, across, q_ref, nk_ref, nv_ref, parents_ref, o_ref, stat_ref, out_ref,
    y_o, y_stat, held_o, held_stat, z_o, z_stat,
    yo_send, yo_receive, ys_send, ys_receive, zo_send, zo_receive, zs_send, zs_receive,
):
    rank = lax.axis_index("tensor")
    z, y = rank // across, lax.rem(rank, across)
    greet(deep, across, z, y)
    requests, nodes, width = q_ref.shape
    along_y, along_z = [], []
    for dz in [*range(1, deep), 0]:
        slots = []
        for dy in range(1, across):
            other = lax.rem(y + dy, across)
            slot = lax.rem(z + dz, deep) * across + other
            at = (dz, dy - 1)
            device = peer(z, other, across)
            pair = (
                remote(o_ref.at[slot], y_o.at[at], yo_send, yo_receive, at, device),
                remote(stat_ref.at[slot], y_stat.at[at], ys_send, ys_receive, at, device),
            )
            for copy in pair:
                copy.start()
            slots.append(pair)
        along_y.append((dz, slots))
    for dz, slots in along_y:
        for pair in slots:
            for copy in pair:
                copy.wait_recv()
        mine = lax.rem(z + dz, deep) * across + y
        for r in range(requests):
            parts = [(stat_ref[mine, r, 0:1], stat_ref[mine, r, 1:2], o_ref[mine, r])]
            for dy in range(1, across):
                got = y_stat.at[dz, dy - 1]
                parts.append((got[r, 0:1], got[r, 1:2], y_o[dz, dy - 1, r]))
            best, whole, mean = combine(parts)
            held_o[dz, r] = mean.astype(held_o.dtype)
            held_stat[dz, r, 0:1] = best
            held_stat[dz, r, 1:2] = whole
        if dz:
            device = peer(lax.rem(z + dz, deep), y, across)
            at = (dz - 1,)
            pair = (
                remote(held_o.at[dz], z_o.at[at], zo_send, zo_receive, at, device),
                remote(held_stat.at[dz], z_stat.at[at], zs_send, zs_receive, at, device),
            )
            for copy in pair:
                copy.start()
            along_z.append(pair)
    trees = [
        tree_part(head_rows(q_ref[r]), nk_ref[r], nv_ref[r], parents_ref[r])
        for r in range(requests)
    ]
    for pair in along_z:
        for copy in pair:
            copy.wait_recv()
    for r in range(requests):
        parts = [trees[r], (held_stat[0, r, 0:1], held_stat[0, r, 1:2], held_o[0, r])]
        for at in range(deep - 1):
            parts.append((z_stat[at, r, 0:1], z_stat[at, r, 1:2], z_o[at, r]))
        joined = combine(parts)[2].T.astype(out_ref.dtype)
        for h in range(width // HEAD_SIZE):
            out_ref[r, :, h * HEAD_SIZE : (h + 1) * HEAD_SIZE] = joined[
                h * nodes : (h + 1) * nodes
            ]
    for dz, slots in along_y:
        for pair in slots:
            for copy in pair:
                copy.wait_send()
    for pair in along_z:
        for copy in pair:
            copy.wait_send()


def join(queries, node_keys, node_values, parents, outs, stats):
    ranks = outs.shape[0]
    deep = 4
    across = ranks // deep
    block, stat = outs.shape[1:], stats.shape[1:]
    semaphore = pltpu.SemaphoreType.DMA
    by_y, by_z = (deep, across - 1), (deep - 1,)
    return pl.pallas_call(
        functools.partial(join_kernel, deep, across),
        in_specs=[pl.BlockSpec(memory_space=pltpu.VMEM)] * 6,
        out_specs=pl.BlockSpec(memory_space=pltpu.VMEM),
        out_shape=jax.ShapeDtypeStruct(queries.shape, jnp.bfloat16),
        scratch_shapes=[
            pltpu.VMEM(by_y + block, jnp.bfloat16),
            pltpu.VMEM(by_y + stat, jnp.float32),
            pltpu.VMEM((deep,) + block, jnp.bfloat16),
            pltpu.VMEM((deep,) + stat, jnp.float32),
            pltpu.VMEM(by_z + block, jnp.bfloat16),
            pltpu.VMEM(by_z + stat, jnp.float32),
        ]
        + [semaphore(by_y)] * 4
        + [semaphore(by_z)] * 4,
        compiler_params=pltpu.CompilerParams(
            collective_id=1, has_side_effects=True, vmem_limit_bytes=40 << 20
        ),
    )(queries, node_keys, node_values, parents[:, None, :], outs, stats)


def per_device(queries, stored_keys, stored_values, node_keys, node_values, parents, lengths):
    ranks = lax.axis_size("tensor")
    rank = lax.axis_index("tensor")
    extent = stored_keys.shape[1]
    every = gather(queries, ranks)
    first = (rank * extent).astype(jnp.int32)[None]
    outs, stats = block_attention(every, stored_keys, stored_values, first, lengths)
    group = rank * KEY_VALUE_HEADS // ranks
    own_keys = lax.dynamic_slice_in_dim(node_keys, group * HEAD_SIZE, HEAD_SIZE, 2)
    own_values = lax.dynamic_slice_in_dim(node_values, group * HEAD_SIZE, HEAD_SIZE, 2)
    attended = join(queries, own_keys, own_values, parents, outs, stats)
    length = lax.axis_size("pipe")
    return lax.ppermute(attended, "pipe", [(i, (i + 1) % length) for i in range(length)])


def solution(mesh):
    placed = (
        P("pipe", None, "tensor"),
        P("pipe", "tensor", None),
        P("pipe", "tensor", None),
        P("pipe", None, None),
        P("pipe", None, None),
        P("pipe", None),
        P("pipe"),
    )
    return jax.shard_map(
        per_device, mesh=mesh, in_specs=placed, out_specs=P("pipe", None, "tensor"), check_vma=False
    )
```

```python
import functools

import jax
import jax.numpy as jnp
from jax import lax
from jax.experimental import pallas as pl
from jax.experimental.pallas import tpu as pltpu
from jax.sharding import PartitionSpec as P

QUERY_HEADS = 128
KEY_VALUE_HEADS = 8
HEAD_SIZE = 128
MASKED_SCORE = -1e30
LOG2_E = 1.4426950408889634
NT = (((1,), (1,)), ((), ()))
TN = (((0,), (0,)), ((), ()))


def head_rows(block):
    heads = block.shape[1] // HEAD_SIZE
    return jnp.concatenate(
        [block[:, h * HEAD_SIZE : (h + 1) * HEAD_SIZE] for h in range(heads)], axis=0
    )


def tree_part(rows, node_keys, node_values, parents):
    nodes = node_keys.shape[0]
    row = lax.broadcasted_iota(jnp.int32, (nodes, nodes), 0)
    column = lax.broadcasted_iota(jnp.int32, (nodes, nodes), 1)
    reached = ((parents == row) | (row == column)).astype(jnp.bfloat16)
    for squaring in range(nodes.bit_length()):
        product = jnp.dot(reached, reached, preferred_element_type=jnp.float32)
        reached = (product > 0.5).astype(jnp.bfloat16)
    width = rows.shape[0]
    node = lax.broadcasted_iota(jnp.int32, (nodes, width), 0)
    owner = lax.rem(lax.broadcasted_iota(jnp.int32, (nodes, width), 1), nodes)
    spread = (node == owner).astype(jnp.bfloat16)
    allowed = jnp.dot(reached, spread, preferred_element_type=jnp.float32) > 0.5
    scores = lax.dot_general(node_keys, rows, NT, preferred_element_type=jnp.float32)
    scores = jnp.where(allowed, scores * HEAD_SIZE**-0.5, MASKED_SCORE)
    top = jnp.max(scores, axis=0, keepdims=True)
    weights = jnp.where(allowed, jnp.exp(scores - top), 0.0)
    total = jnp.sum(weights, axis=0, keepdims=True)
    out = lax.dot_general(
        node_values, weights.astype(jnp.bfloat16), TN, preferred_element_type=jnp.float32
    )
    return top, total, out / total


def peer(z, y, across):
    return {"tensor": z * across + y}


def remote(source, target, sends, receives, at, device):
    return pltpu.make_async_remote_copy(
        src_ref=source,
        dst_ref=target,
        send_sem=sends.at[at],
        recv_sem=receives.at[at],
        device_id=device,
        device_id_type=pl.DeviceIdType.MESH,
    )


def greet(deep, across, z, y):
    barrier = pltpu.get_barrier_semaphore()
    partners = [peer(lax.rem(z + dz, deep), y, across) for dz in range(1, deep)]
    partners += [peer(z, lax.rem(y + dy, across), across) for dy in range(1, across)]
    for partner in partners:
        pl.semaphore_signal(
            barrier, inc=1, device_id=partner, device_id_type=pl.DeviceIdType.MESH
        )
    pl.semaphore_wait(barrier, len(partners))


def block_part(live, source, keys, values, o_ref, stat_ref):
    positions = lax.broadcasted_iota(jnp.int32, (keys.shape[0], 1), 0)
    active = positions < live
    scale = HEAD_SIZE**-0.5
    nodes, width = source.shape
    heads = 4
    chunks = width // (heads * HEAD_SIZE)

    def chunk(c):
        across = pl.ds(pl.multiple_of(c * heads * HEAD_SIZE, heads * HEAD_SIZE), heads * HEAD_SIZE)
        columns = pl.ds(pl.multiple_of(c * heads * nodes, heads * nodes), heads * nodes)
        rows = head_rows(source[:, across])
        scores = lax.dot_general(keys[...], rows, NT, preferred_element_type=jnp.float32)
        scores = jnp.where(active, scores, MASKED_SCORE)
        top = jnp.max(scores, axis=0, keepdims=True)
        weights = jnp.exp2((scores - top) * (scale * LOG2_E))
        total = jnp.sum(weights, axis=0, keepdims=True)
        out = lax.dot_general(
            values[...], weights.astype(jnp.bfloat16), TN, preferred_element_type=jnp.float32
        )
        o_ref[:, columns] = (out / total).astype(jnp.bfloat16)
        stat_ref[0:1, columns] = top * scale
        stat_ref[1:2, columns] = total

    @pl.loop(0, chunks // 2)
    def _(step):
        chunk(2 * step)
        chunk(2 * step + 1)


def block_kernel(
    deep, across, lengths_ref, q_ref, k_ref, v_ref, o_ref, stat_ref,
    every_ref, z_send, z_receive, y_send, y_receive,
):
    rank = lax.axis_index("tensor")
    z, y = rank // across, lax.rem(rank, across)
    share = deep * across // KEY_VALUE_HEADS
    requests = q_ref.shape[0]
    extent = k_ref.shape[1]
    greet(deep, across, z, y)
    along_z, along_y = {}, {}

    def send_y(source, slot, r, dz):
        for dy in range(1, across):
            at = (r, dz, dy - 1)
            device = peer(z, lax.rem(y + dy, across), across)
            copy = remote(source, every_ref.at[slot, r], y_send, y_receive, at, device)
            copy.start()
            along_y[at] = copy

    for r in range(requests):
        for dz in range(1, deep):
            at = (r, dz - 1)
            device = peer(lax.rem(z + dz, deep), y, across)
            copy = remote(q_ref.at[r], every_ref.at[rank, r], z_send, z_receive, at, device)
            copy.start()
            along_z[at] = copy
        send_y(q_ref.at[r], rank, r, 0)

    def work(source, slot, r):
        columns = pl.ds(pl.multiple_of(slot // share * HEAD_SIZE, HEAD_SIZE), HEAD_SIZE)
        block_part(
            lengths_ref[r] - rank * extent,
            source,
            k_ref.at[r, :, columns],
            v_ref.at[r, :, columns],
            o_ref.at[slot, r],
            stat_ref.at[slot, r],
        )

    def pass_on(r, dz):
        along_z[r, dz - 1].wait_recv()
        slot = lax.rem(z + deep - dz, deep) * across + y
        send_y(every_ref.at[slot, r], slot, r, dz)
        work(every_ref.at[slot, r], slot, r)

    def from_y(r, dz):
        for dy in range(1, across):
            along_y[r, dz, dy - 1].wait_recv()
            other = lax.rem(y + across - dy, across)
            slot = lax.rem(z + deep - dz, deep) * across + other
            work(every_ref.at[slot, r], slot, r)

    for r in range(requests):
        work(q_ref.at[r], rank, r)
    for r in range(requests):
        from_y(r, 0)
    for dz in range(1, deep):
        pass_on(0, dz)
    for r in range(1, requests):
        for dz in range(1, deep):
            pass_on(r, dz)
            from_y(r - 1, dz)
    for dz in range(1, deep):
        from_y(requests - 1, dz)
    for copy in [*along_z.values(), *along_y.values()]:
        copy.wait_send()


def block_attention(queries, keys, values, lengths, ranks):
    requests, nodes, width = queries.shape
    deep = 4
    across = ranks // deep
    rows = width // HEAD_SIZE * nodes
    semaphore = pltpu.SemaphoreType.DMA
    vmem = pl.BlockSpec(memory_space=pltpu.VMEM)
    return pl.pallas_call(
        functools.partial(block_kernel, deep, across),
        in_specs=[pl.BlockSpec(memory_space=pltpu.SMEM), vmem, vmem, vmem],
        out_specs=[vmem, vmem],
        out_shape=[
            jax.ShapeDtypeStruct((ranks, requests, HEAD_SIZE, rows), jnp.bfloat16),
            jax.ShapeDtypeStruct((ranks, requests, 2, rows), jnp.float32),
        ],
        scratch_shapes=[
            pltpu.VMEM((ranks,) + queries.shape, queries.dtype),
            semaphore((requests, deep - 1)),
            semaphore((requests, deep - 1)),
            semaphore((requests, deep, across - 1)),
            semaphore((requests, deep, across - 1)),
        ],
        compiler_params=pltpu.CompilerParams(
            collective_id=0, has_side_effects=True, vmem_limit_bytes=48 << 20
        ),
    )(lengths, queries, keys, values)


def combine(parts):
    best = functools.reduce(jnp.maximum, [top for top, total, mean in parts])
    shares = [total * jnp.exp(top - best) for top, total, mean in parts]
    whole = sum(shares[1:], shares[0])
    mean = sum(
        (share / whole) * part[2].astype(jnp.float32) for share, part in zip(shares, parts)
    )
    return best, whole, mean


def join_kernel(
    deep, across, q_ref, nk_ref, nv_ref, parents_ref, o_ref, stat_ref, out_ref,
    y_o, y_stat, held_o, held_stat, z_o, z_stat,
    yo_send, yo_receive, ys_send, ys_receive, zo_send, zo_receive, zs_send, zs_receive,
):
    rank = lax.axis_index("tensor")
    z, y = rank // across, lax.rem(rank, across)
    greet(deep, across, z, y)
    requests, nodes, width = q_ref.shape
    along_y, along_z = [], []
    for dz in [*range(1, deep), 0]:
        slots = []
        for dy in range(1, across):
            other = lax.rem(y + dy, across)
            slot = lax.rem(z + dz, deep) * across + other
            at = (dz, dy - 1)
            device = peer(z, other, across)
            pair = (
                remote(o_ref.at[slot], y_o.at[at], yo_send, yo_receive, at, device),
                remote(stat_ref.at[slot], y_stat.at[at], ys_send, ys_receive, at, device),
            )
            for copy in pair:
                copy.start()
            slots.append(pair)
        along_y.append((dz, slots))
    for dz, slots in along_y:
        for pair in slots:
            for copy in pair:
                copy.wait_recv()
        mine = lax.rem(z + dz, deep) * across + y
        for r in range(requests):
            parts = [(stat_ref[mine, r, 0:1], stat_ref[mine, r, 1:2], o_ref[mine, r])]
            for dy in range(1, across):
                got = y_stat.at[dz, dy - 1]
                parts.append((got[r, 0:1], got[r, 1:2], y_o[dz, dy - 1, r]))
            best, whole, mean = combine(parts)
            held_o[dz, r] = mean.astype(held_o.dtype)
            held_stat[dz, r, 0:1] = best
            held_stat[dz, r, 1:2] = whole
        if dz:
            device = peer(lax.rem(z + dz, deep), y, across)
            at = (dz - 1,)
            pair = (
                remote(held_o.at[dz], z_o.at[at], zo_send, zo_receive, at, device),
                remote(held_stat.at[dz], z_stat.at[at], zs_send, zs_receive, at, device),
            )
            for copy in pair:
                copy.start()
            along_z.append(pair)
    trees = [
        tree_part(head_rows(q_ref[r]), nk_ref[r], nv_ref[r], parents_ref[r])
        for r in range(requests)
    ]
    for pair in along_z:
        for copy in pair:
            copy.wait_recv()
    for r in range(requests):
        parts = [trees[r], (held_stat[0, r, 0:1], held_stat[0, r, 1:2], held_o[0, r])]
        for at in range(deep - 1):
            parts.append((z_stat[at, r, 0:1], z_stat[at, r, 1:2], z_o[at, r]))
        joined = combine(parts)[2].T.astype(out_ref.dtype)
        for h in range(width // HEAD_SIZE):
            out_ref[r, :, h * HEAD_SIZE : (h + 1) * HEAD_SIZE] = joined[
                h * nodes : (h + 1) * nodes
            ]
    for dz, slots in along_y:
        for pair in slots:
            for copy in pair:
                copy.wait_send()
    for pair in along_z:
        for copy in pair:
            copy.wait_send()


def join(queries, node_keys, node_values, parents, outs, stats):
    ranks = outs.shape[0]
    deep = 4
    across = ranks // deep
    block, stat = outs.shape[1:], stats.shape[1:]
    semaphore = pltpu.SemaphoreType.DMA
    by_y, by_z = (deep, across - 1), (deep - 1,)
    return pl.pallas_call(
        functools.partial(join_kernel, deep, across),
        in_specs=[pl.BlockSpec(memory_space=pltpu.VMEM)] * 6,
        out_specs=pl.BlockSpec(memory_space=pltpu.VMEM),
        out_shape=jax.ShapeDtypeStruct(queries.shape, jnp.bfloat16),
        scratch_shapes=[
            pltpu.VMEM(by_y + block, jnp.bfloat16),
            pltpu.VMEM(by_y + stat, jnp.float32),
            pltpu.VMEM((deep,) + block, jnp.bfloat16),
            pltpu.VMEM((deep,) + stat, jnp.float32),
            pltpu.VMEM(by_z + block, jnp.bfloat16),
            pltpu.VMEM(by_z + stat, jnp.float32),
        ]
        + [semaphore(by_y)] * 4
        + [semaphore(by_z)] * 4,
        compiler_params=pltpu.CompilerParams(
            collective_id=1, has_side_effects=True, vmem_limit_bytes=40 << 20
        ),
    )(queries, node_keys, node_values, parents[:, None, :], outs, stats)


def per_device(queries, stored_keys, stored_values, node_keys, node_values, parents, lengths):
    ranks = lax.axis_size("tensor")
    rank = lax.axis_index("tensor")
    outs, stats = block_attention(queries, stored_keys, stored_values, lengths, ranks)
    group = rank * KEY_VALUE_HEADS // ranks
    own_keys = lax.dynamic_slice_in_dim(node_keys, group * HEAD_SIZE, HEAD_SIZE, 2)
    own_values = lax.dynamic_slice_in_dim(node_values, group * HEAD_SIZE, HEAD_SIZE, 2)
    attended = join(queries, own_keys, own_values, parents, outs, stats)
    length = lax.axis_size("pipe")
    return lax.ppermute(attended, "pipe", [(i, (i + 1) % length) for i in range(length)])


def solution(mesh):
    placed = (
        P("pipe", None, "tensor"),
        P("pipe", "tensor", None),
        P("pipe", "tensor", None),
        P("pipe", None, None),
        P("pipe", None, None),
        P("pipe", None),
        P("pipe"),
    )
    return jax.shard_map(
        per_device, mesh=mesh, in_specs=placed, out_specs=P("pipe", None, "tensor"), check_vma=False
    )
```
